32 devices in a mesh: expert: 16 (over z, y, core), edata: 2 (over x).
Axes of the slice: x: 2, y: 2, z: 4, core: 2. Of those that a mesh axis runs over, the one named last changes fastest.
Arguments:
- tokens: bfloat16 [1024, 2048], P(('expert', 'edata')), may hold values from -6 to 6
- out_grad: bfloat16 [1024, 2048], P(('expert', 'edata')), may hold values from -6 to 6
- routes: int32 [1024, 8], P(('expert', 'edata')), may hold values from 0 to 15, as said below
- gate_codes: int32 [1024, 8], P(('expert', 'edata')), may hold values from 1 to 4095
- w_gate: bfloat16 [16, 2048, 768], P('expert'), may hold values from -0.125 to 0.125
- w_up: bfloat16 [16, 2048, 768], P('expert'), may hold values from -0.125 to 0.125
- w_down: bfloat16 [16, 768, 2048], P('expert'), may hold values from -0.21875 to 0.21875
Outputs:
- mixed: bfloat16 [1024, 2048], P(('expert', 'edata'))
- input_grad: bfloat16 [1024, 2048], P(('expert', 'edata'))
- grad_down: float32 [2048, 16, 768], P('edata', 'expert')
The draws below stay inside these ranges and needn't reach their ends.
Inputs may be any that keep to these rules, and one draw needn't show every extreme that they name: `routes`: each token names 8 different experts. For each index of edata one expert, drawn anew in each draw, is named by exactly 32 of the 32 tokens of every device of that index of edata; any other expert is named by at most (15) tokens of one device.
All inputs are finite; a program needn't handle non-finite values.
Results may differ from the reference program's by a relative error of at most 0.017.
Values may be sent and summed in bfloat16 or wider, within the bound.
No kernel may reach another device: no remote copies, remote signals or barrier semaphores. Data moves between devices by JAX's collectives and lax.ppermute only.
A program may use at most 128 MiB of HBM per device.

```python
import jax
import jax.numpy as jnp
from jax import lax

D = 2048
HID = 768
TOPK = 8
TOK_DEV = 32
BLOCK = 128
EXPERTS = 16
CAP = 32
TOKENS = 1024
N_EDATA = 2


def route_block(block_key, hot_expert):
    perm_key, pick_key, turn_key = jax.random.split(block_key, 3)
    ordering = jax.random.permutation(perm_key, EXPERTS).astype(jnp.int32)
    hot_last = jnp.argsort((ordering == hot_expert).astype(jnp.int32), stable=True)
    others = ordering[hot_last][:EXPERTS - 1]
    chosen = jax.random.permutation(pick_key, TOK_DEV).astype(jnp.int32) < CAP
    takes_hot = chosen.astype(jnp.int32)
    lengths = TOPK - takes_hot
    starts = jnp.cumsum(lengths) - lengths
    columns = jnp.arange(TOPK, dtype=jnp.int32)
    placing = (starts[:, None] + columns[None, :] - takes_hot[:, None]) % (EXPERTS - 1)
    picked = others[placing]
    row_set = jnp.where((columns[None, :] == 0) & chosen[:, None], hot_expert, picked)
    turn_by = jax.random.randint(turn_key, (TOK_DEV,), 0, TOPK).astype(jnp.int32)
    rolled = (columns[None, :] + turn_by[:, None]) % TOPK
    return jnp.take_along_axis(row_set, rolled, axis=1).astype(jnp.int32)


def draw_routes(key, part):
    blocks = TOKENS // TOK_DEV
    hot_all = jax.random.randint(jax.random.fold_in(key, 11), (N_EDATA,), 0, EXPERTS).astype(jnp.int32)
    block_ids = jnp.arange(blocks, dtype=jnp.int32)
    hot_of_block = hot_all[block_ids % N_EDATA]
    block_keys = jax.vmap(lambda block_index: jax.random.fold_in(key, block_index + 100))(block_ids)
    return jax.vmap(route_block)(block_keys, hot_of_block).reshape(TOKENS, TOPK)


def touch_ends(array, stream_key, least, top_value):
    place = [jax.random.randint(jax.random.fold_in(stream_key, axis), (), 0, length) for axis, length in enumerate(array.shape)]
    main_axis = array.shape.index(max(array.shape))
    beside = place[:main_axis] + [(place[main_axis] + 1) % array.shape[main_axis]] + place[main_axis + 1:]
    return array.at[tuple(place)].set(least).at[tuple(beside)].set(top_value)


def shard_levels(own_key, dims, pieces, low, largest):
    factor_of, own = 1.0, jax.random.fold_in(own_key, 6)
    for axis_at, shards_of in pieces:
        steps = jnp.exp(jax.random.uniform(jax.random.fold_in(own, axis_at), (shards_of,), jnp.float32, low / len(pieces), largest / len(pieces)))
        factor_of = factor_of * jnp.repeat(steps, dims[axis_at] // shards_of).reshape([-1 if axis == axis_at else 1 for axis in range(len(dims))])
    return factor_of


def scatter_about(key, extent, deviation, reach, shards=(), kind=jnp.bfloat16):
    gain = shard_levels(key, extent, shards, -0.22, 0.18) if shards else 1.0
    values = jax.random.normal(key, extent, jnp.float32) * deviation * gain
    return jnp.minimum(jnp.maximum(values, -reach), reach).astype(kind)


def setup_inputs(seed: int = 0) -> dict:
    key_of = jax.random.split(jax.random.key(seed), 8)
    tokens = scatter_about(key_of[0], (TOKENS, D), 1.0, 6.0, ((0, 32),))
    out_grad = scatter_about(key_of[1], (TOKENS, D), 1.0, 6.0, ((0, 32),))
    routes = draw_routes(jax.random.fold_in(key_of[7], 71), 0)
    gate_codes = touch_ends(jax.random.randint(key_of[3], (TOKENS, TOPK), 1, 4096), jax.random.fold_in(key_of[3], 1), 1, 4095).astype(jnp.int32)
    w_gate = scatter_about(key_of[4], (EXPERTS, D, HID), D ** -0.5, 0.125, ((0, 16),))
    w_up = scatter_about(key_of[5], (EXPERTS, D, HID), D ** -0.5, 0.125, ((0, 16),))
    w_down = scatter_about(key_of[6], (EXPERTS, HID, D), HID ** -0.5, 0.21875, ((0, 16),))
    return dict(tokens=tokens, out_grad=out_grad, routes=routes, gate_codes=gate_codes, w_gate=w_gate, w_up=w_up, w_down=w_down)


def take_rows(source, row_ids, row_limit):
    is_valid = row_ids < row_limit
    safe_rows = jnp.minimum(row_ids, row_limit - 1).astype(jnp.int32)
    return jnp.where(is_valid[:, None], jnp.take(source, safe_rows, axis=0), jnp.zeros((), source.dtype))


def expert_block(rows_in, grads_in, gate_mat, up_mat, down_mat):
    gate_pre = jnp.dot(rows_in, gate_mat, preferred_element_type=jnp.float32)
    up_pre = jnp.dot(rows_in, up_mat, preferred_element_type=jnp.float32)
    sig_gate = jax.nn.sigmoid(gate_pre)
    act_gate = gate_pre * sig_gate
    hidden_act = (act_gate * up_pre).astype(jnp.bfloat16)
    expert_out = jnp.dot(hidden_act, down_mat, preferred_element_type=jnp.float32).astype(jnp.bfloat16)
    grad_hidden = jnp.dot(grads_in, down_mat.T, preferred_element_type=jnp.float32)
    grad_gate_pre = (grad_hidden * up_pre * sig_gate * (1.0 + gate_pre * (1.0 - sig_gate))).astype(jnp.bfloat16)
    grad_up_pre = (grad_hidden * act_gate).astype(jnp.bfloat16)
    grad_rows = (jnp.dot(grad_gate_pre, gate_mat.T, preferred_element_type=jnp.float32)
                 + jnp.dot(grad_up_pre, up_mat.T, preferred_element_type=jnp.float32)).astype(jnp.bfloat16)
    return expert_out, grad_rows, hidden_act


def add_expert(total_grad, term, expert_id):
    current = lax.dynamic_index_in_dim(total_grad, expert_id, 0, keepdims=False)
    return lax.dynamic_update_index_in_dim(total_grad, current + term, expert_id, 0)


def reference(tokens, out_grad, routes, gate_codes, w_gate, w_up, w_down):
    routed = TOKENS * TOPK
    gate_float = gate_codes.astype(jnp.float32)
    gate_values = gate_float / jnp.sum(gate_float, axis=1, keepdims=True)
    scaled = (gate_values[:, :, None] * out_grad[:, None, :].astype(jnp.float32)).astype(jnp.bfloat16).reshape(routed, D)
    flat_expert = routes.reshape(routed).astype(jnp.int32)
    expert_ids = jnp.arange(EXPERTS, dtype=jnp.int32)
    counts = jnp.sum((flat_expert[:, None] == expert_ids[None, :]).astype(jnp.int32), axis=0)
    padded = (counts + BLOCK - 1) // BLOCK * BLOCK
    begins = jnp.cumsum(padded) - padded
    firsts = jnp.cumsum(counts) - counts
    sorted_order = jnp.argsort(flat_expert, stable=True).astype(jnp.int32)
    sorted_expert = flat_expert[sorted_order]
    place_sorted = (begins[sorted_expert] + jnp.arange(routed, dtype=jnp.int32) - firsts[sorted_expert]).astype(jnp.int32)
    block_count = routed // BLOCK + EXPERTS
    slot_total = block_count * BLOCK
    source_of = jnp.full((slot_total,), routed, jnp.int32).at[place_sorted].set(sorted_order)
    place_of = jnp.zeros((routed,), jnp.int32).at[sorted_order].set(place_sorted)
    block_starts = jnp.arange(block_count, dtype=jnp.int32) * BLOCK
    block_expert = jnp.clip(jnp.sum((begins[None, :] <= block_starts[:, None]).astype(jnp.int32), axis=1) - 1, 0, EXPERTS - 1).astype(jnp.int32)
    token_of = jnp.where(source_of < routed, source_of // TOPK, TOKENS).astype(jnp.int32)

    def block_step(sum_down, block_input):
        row_ids, token_ids, expert_id = block_input
        rows_in = take_rows(tokens, token_ids, TOKENS)
        grads_in = take_rows(scaled, row_ids, routed)
        gate_mat = lax.dynamic_index_in_dim(w_gate, expert_id, 0, keepdims=False)
        up_mat = lax.dynamic_index_in_dim(w_up, expert_id, 0, keepdims=False)
        down_mat = lax.dynamic_index_in_dim(w_down, expert_id, 0, keepdims=False)
        expert_out, grad_rows, hidden_act = expert_block(rows_in, grads_in, gate_mat, up_mat, down_mat)
        sum_down = add_expert(sum_down, jnp.dot(grads_in.T, hidden_act, preferred_element_type=jnp.float32), expert_id)
        return sum_down, (expert_out, grad_rows)

    zero_grad = jnp.zeros((EXPERTS, D, HID), jnp.float32)
    sum_down, outputs = lax.scan(block_step, zero_grad,
                                 (source_of.reshape(block_count, BLOCK), token_of.reshape(block_count, BLOCK), block_expert))
    out_flat = outputs[0].reshape(slot_total, D)
    grad_flat = outputs[1].reshape(slot_total, D)
    rows_out = jnp.take(out_flat, place_of, axis=0).reshape(TOKENS, TOPK, D)
    rows_grad = jnp.take(grad_flat, place_of, axis=0).reshape(TOKENS, TOPK, D)
    mixed = jnp.sum(gate_values[:, :, None] * rows_out.astype(jnp.float32), axis=1).astype(jnp.bfloat16)
    input_grad = jnp.sum(rows_grad.astype(jnp.float32), axis=1).astype(jnp.bfloat16)
    grad_down = jnp.transpose(sum_down, (1, 0, 2))
    return (mixed, input_grad, grad_down)
```

```python
import jax
import jax.numpy as jnp
from jax import lax
from jax.sharding import PartitionSpec as P

LANES = 128


def swap(value, axis, distance):
    size = lax.axis_size(axis)
    return lax.ppermute(value, axis, [(i, i ^ distance) for i in range(size)])


def far_steps(n_expert):
    return list(range(8, n_expert, 4))


def gather_near(block):
    beside = swap(block, "expert", 2)
    own = jnp.concatenate([block, beside], axis=0)
    near = swap(own, "expert", 4)
    return jnp.concatenate([own, near], axis=0)


def gather_far(block, n_expert):
    straight = [swap(block, "expert", step) for step in far_steps(n_expert)]
    straight = jnp.concatenate(straight, axis=0)
    across = swap(straight, "expert", 2)
    return jnp.concatenate([straight, across], axis=0)


def gather_even(block, n_expert):
    return [gather_near(block), gather_far(block, n_expert)]


def gather_odd(parts):
    return [swap(part, "expert", 1) for part in parts]


def scatter_sum(partial, n_expert):
    total_rows, width = partial.shape
    rows = total_rows // n_expert
    half = total_rows // 2
    kept, sent = partial[:half], partial[half:]
    even = (kept + swap(sent, "expert", 1)).reshape(n_expert // 2, rows, width)
    near, far = even[:4], even[4:]
    n_far = far.shape[0] // 2
    from_near = swap(near[2:].reshape(2 * rows, width), "expert", 4).reshape(2, rows, width)
    across = swap(far[n_far:].reshape(n_far * rows, width), "expert", 2).reshape(n_far, rows, width)
    straight = far[:n_far] + across
    beside = swap(near[1] + from_near[1], "expert", 2)
    total = near[0].astype(jnp.float32) + from_near[0].astype(jnp.float32)
    for index, step in enumerate(far_steps(n_expert)):
        total = total + swap(straight[index], "expert", step).astype(jnp.float32)
    total = total + beside.astype(jnp.float32)
    return total.astype(jnp.bfloat16)


def gate_lanes(routes, gate_codes, n_expert):
    experts = jnp.arange(n_expert, dtype=jnp.int32)
    chosen = routes[:, :, None] == experts[None, None, :]
    codes = jnp.sum(jnp.where(chosen, gate_codes[:, :, None], 0), axis=1)
    total = jnp.sum(gate_codes, axis=1, keepdims=True)
    digits = jnp.concatenate([codes // 64, codes % 64, total // 256, total % 256], axis=1)
    return jnp.pad(digits, ((0, 0), (0, LANES - digits.shape[1]))).astype(jnp.bfloat16)


def gate_of_expert(lanes, expert, n_expert):
    values = lanes.astype(jnp.float32)
    index = lax.broadcasted_iota(jnp.int32, values.shape, 1)
    pick = lambda at: jnp.sum(jnp.where(index == at, values, 0.0), axis=1, keepdims=True)
    code = pick(expert) * 64.0 + pick(expert + n_expert)
    total = pick(2 * n_expert) * 256.0 + pick(2 * n_expert + 1)
    return code / total


def dot(left, right, contract):
    return lax.dot_general(left, right, (contract, ((), ())), preferred_element_type=jnp.float32)


def shards(tokens, out_grad, routes, gate_codes, w_gate, w_up, w_down):
    rows, width = tokens.shape
    n_expert = lax.axis_size("expert")
    n_edata = lax.axis_size("edata")
    expert = lax.axis_index("expert")
    gate_mat, up_mat, down_mat = w_gate[0], w_up[0], w_down[0]

    lanes = gate_lanes(routes, gate_codes, n_expert)
    even = gather_even(jnp.concatenate([tokens, lanes], axis=1), n_expert)
    odd = gather_odd(even)
    grads_even = gather_even(out_grad, n_expert)
    grads_odd = gather_odd(grads_even)

    gathered = jnp.concatenate(even + odd, axis=0)
    rows_in, lanes_in = gathered[:, :width], gathered[:, width:]
    gate = gate_of_expert(lanes_in, expert, n_expert)
    gate_pre = dot(rows_in, gate_mat, ((1,), (0,)))
    up_pre = dot(rows_in, up_mat, ((1,), (0,)))
    sig_gate = jax.nn.sigmoid(gate_pre)
    act_gate = gate_pre * sig_gate * gate
    hidden = (act_gate * up_pre).astype(jnp.bfloat16)
    slope = gate * up_pre * sig_gate * (1.0 + gate_pre * (1.0 - sig_gate))
    mixed = scatter_sum(dot(hidden, down_mat, ((1,), (0,))).astype(jnp.bfloat16), n_expert)

    grads_in = jnp.concatenate(grads_even + grads_odd, axis=0)
    grad_hidden = dot(grads_in, down_mat, ((1,), (1,)))
    grad_gate_pre = (grad_hidden * slope).astype(jnp.bfloat16)
    grad_up_pre = (grad_hidden * act_gate).astype(jnp.bfloat16)
    grad_rows = dot(grad_gate_pre, gate_mat, ((1,), (1,))) + dot(grad_up_pre, up_mat, ((1,), (1,)))
    input_grad = scatter_sum(grad_rows.astype(jnp.bfloat16), n_expert)

    place = lax.axis_index("edata")
    share = width // n_edata
    half = grads_in.shape[0] // 2
    grad_down = dot(lax.dynamic_slice_in_dim(grads_in, place * share, share, 1), hidden, ((0,), (0,)))
    for step in range(1, n_edata):
        hidden_other = swap(hidden, "edata", step)
        wanted = lax.dynamic_slice_in_dim(grads_in[:half], (place ^ step) * share, share, 1)
        other_even = swap(wanted, "edata", step)
        other_odd = swap(other_even, "expert", 1)
        grads_other = jnp.concatenate([other_even, other_odd], axis=0)
        grad_down = grad_down + dot(grads_other, hidden_other, ((0,), (0,)))
    return mixed, input_grad, grad_down[:, None, :]


def solution(mesh):
    by_token = P(("expert", "edata"), None)
    by_expert = P("expert", None, None)
    return jax.shard_map(
        shards,
        mesh=mesh,
        in_specs=(by_token,) * 4 + (by_expert,) * 3,
        out_specs=(by_token, by_token, P("edata", "expert", None)),
        check_vma=False,
    )
```

```python
import functools

import jax
import jax.numpy as jnp
from jax import lax
from jax.experimental import pallas as pl
from jax.experimental.pallas import tpu as pltpu
from jax.sharding import PartitionSpec as P

LANES = 128
SHARE_TILE = 256


def swap(value, axis, distance):
    size = lax.axis_size(axis)
    return lax.ppermute(value, axis, [(i, i ^ distance) for i in range(size)])


def after(value, *earlier):
    return lax.optimization_barrier((value,) + earlier)[0]


def far_steps(n_expert):
    return list(range(8, n_expert, 4))


def join(*blocks):
    return jnp.concatenate(blocks, axis=0)


def after_all(values, *earlier):
    return lax.optimization_barrier(tuple(values) + earlier)[:len(values)]


class Near:
    def __init__(self, partial):
        self.half, self.rows = partial.shape[0] // 2, partial.shape[0] // 8
        self.kept = partial[:self.half]
        self.sent = swap(partial[self.half:], "expert", 1)

    def core(self, *earlier):
        kept, sent = after_all([self.kept, self.sent], *earlier)
        self.even = kept + sent
        self.from_near = swap(self.even[2 * self.rows:], "expert", 4)

    def pair(self, *earlier):
        even, from_near = after_all([self.even, self.from_near], *earlier)
        self.ready = even[self.rows:2 * self.rows] + from_near[self.rows:]
        self.beside = swap(self.ready, "expert", 2)

    def total(self):
        own, near = self.even[:self.rows], self.from_near[:self.rows]
        return own.astype(jnp.float32) + near.astype(jnp.float32) + self.beside.astype(jnp.float32)


class Far:
    def __init__(self, partial, n_expert):
        self.steps = far_steps(n_expert)
        self.half, self.quarter = partial.shape[0] // 2, partial.shape[0] // 4
        self.kept = partial[:self.half]
        self.sent = swap(partial[self.half:], "expert", 1)

    def core(self, *earlier):
        kept, sent = after_all([self.kept, self.sent], *earlier)
        self.even = kept + sent
        self.crossed = swap(self.even[self.quarter:], "expert", 2)

    def across(self, *earlier):
        even, crossed = after_all([self.even, self.crossed], *earlier)
        self.ready = even[:self.quarter] + crossed
        rows = self.quarter // len(self.steps)
        self.straight = [swap(self.ready[i * rows:(i + 1) * rows], "expert", step) for i, step in enumerate(self.steps)]

    def total(self):
        return sum(part.astype(jnp.float32) for part in self.straight)


def gate_lanes(routes, gate_codes, n_expert):
    experts = jnp.arange(n_expert, dtype=jnp.int32)
    chosen = routes[:, :, None] == experts[None, None, :]
    codes = jnp.sum(jnp.where(chosen, gate_codes[:, :, None], 0), axis=1)
    total = jnp.sum(gate_codes, axis=1, keepdims=True)
    digits = jnp.concatenate([codes // 64, codes % 64, total // 256, total % 256], axis=1)
    return jnp.pad(digits, ((0, 0), (0, LANES - digits.shape[1]))).astype(jnp.bfloat16)


def gate_of_expert(lanes, expert, n_expert):
    values = lanes.astype(jnp.float32)
    index = lax.broadcasted_iota(jnp.int32, values.shape, 1)
    pick = lambda at: jnp.sum(jnp.where(index == at, values, 0.0), axis=1, keepdims=True)
    code = pick(expert) * 64.0 + pick(expert + n_expert)
    total = pick(2 * n_expert) * 256.0 + pick(2 * n_expert + 1)
    return code / total


def dot(left, right, contract):
    return lax.dot_general(left, right, (contract, ((), ())), preferred_element_type=jnp.float32)


def forward(piece, width, expert, n_expert, gate_mat, up_mat, down_mat):
    rows_in, lanes_in = piece[:, :width], piece[:, width:]
    gate = gate_of_expert(lanes_in, expert, n_expert)
    gate_pre = dot(rows_in, gate_mat, ((1,), (0,)))
    up_pre = dot(rows_in, up_mat, ((1,), (0,)))
    sig_gate = jax.nn.sigmoid(gate_pre)
    act_gate = gate_pre * sig_gate * gate
    hidden = (act_gate * up_pre).astype(jnp.bfloat16)
    slope = gate * up_pre * sig_gate * (1.0 + gate_pre * (1.0 - sig_gate))
    out = dot(hidden, down_mat, ((1,), (0,))).astype(jnp.bfloat16)
    return hidden, act_gate, slope, out


def backward(grads_in, act_gate, slope, gate_mat, up_mat, down_mat):
    grad_hidden = dot(grads_in, down_mat, ((1,), (1,)))
    grad_gate_pre = (grad_hidden * slope).astype(jnp.bfloat16)
    grad_up_pre = (grad_hidden * act_gate).astype(jnp.bfloat16)
    grad_rows = dot(grad_gate_pre, gate_mat, ((1,), (1,))) + dot(grad_up_pre, up_mat, ((1,), (1,)))
    return grad_rows.astype(jnp.bfloat16)


def share_kernel(count, place_ref, *refs):
    out_ref = refs[-1]
    total = None
    for index in range(count):
        grads, hidden = refs[2 * index][...], refs[2 * index + 1][...]
        term = dot(grads, hidden, ((0,), (0,)))
        total = term if total is None else total + term
    out_ref[...] = total[:, None, :]


def weight_share(place, share, own, others):
    tiles = share // SHARE_TILE
    specs, operands = [], []
    for grads, hidden in own:
        specs.append(pl.BlockSpec((grads.shape[0], SHARE_TILE), lambda i, at: (0, at[0] * tiles + i)))
        specs.append(pl.BlockSpec(hidden.shape, lambda i, at: (0, 0)))
        operands += [grads, hidden]
    for grads, hidden in others:
        specs.append(pl.BlockSpec((grads.shape[0], SHARE_TILE), lambda i, at: (0, i)))
        specs.append(pl.BlockSpec(hidden.shape, lambda i, at: (0, 0)))
        operands += [grads, hidden]
    units = operands[1].shape[1]
    rows = sum(grads.shape[0] for grads, _ in own + others)
    return pl.pallas_call(
        functools.partial(share_kernel, len(own) + len(others)),
        out_shape=jax.ShapeDtypeStruct((share, 1, units), jnp.float32),
        grid_spec=pltpu.PrefetchScalarGridSpec(
            num_scalar_prefetch=1,
            grid=(tiles,),
            in_specs=specs,
            out_specs=pl.BlockSpec((SHARE_TILE, 1, units), lambda i, at: (i, 0, 0)),
        ),
        compiler_params=pltpu.CompilerParams(vmem_limit_bytes=40 * 1024 * 1024),
        cost_estimate=pl.CostEstimate(flops=2 * share * units * rows, bytes_accessed=4 * share * units + 2 * rows * (share + units), transcendentals=0),
    )(jnp.reshape(place, (1,)).astype(jnp.int32), *operands)


def shards(tokens, out_grad, routes, gate_codes, w_gate, w_up, w_down):
    rows, width = tokens.shape
    n_expert = lax.axis_size("expert")
    n_edata = lax.axis_size("edata")
    expert = lax.axis_index("expert")
    place = lax.axis_index("edata")
    share = width // n_edata
    gate_mat, up_mat, down_mat = w_gate[0], w_up[0], w_down[0]
    steps = far_steps(n_expert)

    mats = (gate_mat, up_mat, down_mat)
    block = jnp.concatenate([tokens, gate_lanes(routes, gate_codes, n_expert)], axis=1)
    straight = [swap(block, "expert", step) for step in steps]
    pair = join(block, swap(block, "expert", 2))
    near = swap(pair, "expert", 4)
    grad_beside = swap(after(out_grad, pair), "expert", 2)
    far_straight = join(*after_all(straight, pair))
    across = swap(far_straight, "expert", 2)
    near_even = join(*after_all([pair, near], far_straight))
    near_odd = swap(near_even, "expert", 1)
    grad_block = after(out_grad, near_even)
    grad_straight = [swap(grad_block, "expert", step) for step in steps]
    grad_pair = join(*after_all([out_grad, grad_beside], near_even))
    grad_near = swap(grad_pair, "expert", 4)

    hidden_n, act_n, slope_n, out_n = forward(join(*after_all([near_even, near_odd], grad_pair)), width, expert, n_expert, *mats)
    far_even = join(*after_all([far_straight, across], out_n))
    far_odd = swap(far_even, "expert", 1)
    mixed_n = Near(out_n)
    mixed_n.core(far_even)
    hidden_f, act_f, slope_f, out_f = forward(join(*after_all([far_even, far_odd], mixed_n.even)), width, expert, n_expert, *mats)
    mixed_f = Far(out_f, n_expert)

    grad_far_straight = join(*after_all(grad_straight, out_f))
    grad_across = swap(grad_far_straight, "expert", 2)
    mixed_f.core(grad_far_straight)
    grad_near_even = join(*after_all([grad_pair, grad_near], mixed_f.even))
    grad_near_odd = swap(grad_near_even, "expert", 1)
    mixed_n.pair(grad_near_even)
    grads_n = join(*after_all([grad_near_even, grad_near_odd], mixed_n.ready))
    rows_n = backward(grads_n, act_n, slope_n, *mats)
    input_n = Near(rows_n)
    grad_far_even = join(*after_all([grad_far_straight, grad_across], rows_n))
    grad_far_odd = swap(grad_far_even, "expert", 1)
    mixed_f.across(grad_far_even)
    input_n.core(mixed_f.ready)
    grads_f = join(*after_all([grad_far_even, grad_far_odd], input_n.even))
    rows_f = backward(grads_f, act_f, slope_f, *mats)
    input_f = Far(rows_f, n_expert)
    input_n.pair(rows_f)
    input_f.core(input_n.ready)
    input_f.across(input_f.even)

    others = []
    for step in range(1, n_edata):
        there = (place ^ step) * share
        for hidden, even in ((hidden_n, grad_near_even), (hidden_f, grad_far_even)):
            hidden_other = swap(hidden, "edata", step)
            other_even = swap(lax.dynamic_slice_in_dim(even, there, share, 1), "edata", step)
            others.append((join(other_even, swap(other_even, "expert", 1)), hidden_other))
    grad_down = weight_share(place, share, [(grads_n, hidden_n), (grads_f, hidden_f)], others)
    mixed = (mixed_n.total() + mixed_f.total()).astype(jnp.bfloat16)
    input_grad = (input_n.total() + input_f.total()).astype(jnp.bfloat16)
    return mixed, input_grad, grad_down


def solution(mesh):
    by_token = P(("expert", "edata"), None)
    by_expert = P("expert", None, None)
    return jax.shard_map(
        shards,
        mesh=mesh,
        in_specs=(by_token,) * 4 + (by_expert,) * 3,
        out_specs=(by_token, by_token, P("edata", "expert", None)),
        check_vma=False,
    )
```

```python
import functools

import jax
import jax.numpy as jnp
from jax import lax
from jax.experimental import pallas as pl
from jax.experimental.pallas import tpu as pltpu
from jax.sharding import PartitionSpec as P

TILE = 256
OUT_TILE = 512
SHARE_TILE = 256
LANES = 128
LIMIT = 12 * 1024 * 1024
BF16 = jnp.bfloat16
F32 = jnp.float32


def swap(value, axis, distance):
    size = lax.axis_size(axis)
    return lax.ppermute(value, axis, [(i, i ^ distance) for i in range(size)])


def after(value, *earlier):
    return lax.optimization_barrier((value,) + earlier)[0]


def after_all(values, *earlier):
    return lax.optimization_barrier(tuple(values) + earlier)[: len(values)]


def dot(left, right, contract):
    return lax.dot_general(left, right, (contract, ((), ())), preferred_element_type=F32)


class Order:
    def __init__(self, first):
        self.last = first

    def __call__(self, function, *operands):
        operands = lax.optimization_barrier((*operands, self.last))[:-1]
        result = function(*operands)
        self.last = result[0] if isinstance(result, (tuple, list)) else result
        return result


def gate_lanes(routes, gate_codes, n_expert):
    experts = jnp.arange(n_expert, dtype=jnp.int32)
    chosen = routes[:, :, None] == experts[None, None, :]
    codes = jnp.sum(jnp.where(chosen, gate_codes[:, :, None], 0), axis=1)
    total = jnp.sum(gate_codes, axis=1, keepdims=True)
    digits = jnp.concatenate([codes >> 6, codes & 63, total >> 8, total & 255], axis=1)
    return jnp.pad(digits, ((0, 0), (0, LANES - digits.shape[1]))).astype(BF16)


def block_kernel(first_ref, own_ref, got_ref, lanes_ref, out_ref):
    rows, width = own_ref.shape

    def fill(own, got):
        out_ref[own, :width] = own_ref[...]
        out_ref[got, :width] = got_ref[...]
        out_ref[own, width:] = lanes_ref[...]
        out_ref[got, width:] = jnp.zeros(lanes_ref.shape, BF16)

    choose(first_ref[0], fill, slice(0, rows), slice(rows, 2 * rows))


def make_block(first, own, got, lanes):
    rows, width = own.shape
    vmem = pl.BlockSpec(memory_space=pltpu.VMEM)
    return pl.pallas_call(
        block_kernel,
        out_shape=jax.ShapeDtypeStruct((2 * rows, width + LANES), BF16),
        in_specs=[pl.BlockSpec(memory_space=pltpu.SMEM)] + [vmem] * 3,
        out_specs=vmem,
        compiler_params=pltpu.CompilerParams(vmem_limit_bytes=4 * 1024 * 1024),
        cost_estimate=pl.CostEstimate(flops=10**6, bytes_accessed=10**6, transcendentals=0),
    )(first, own, got, lanes)


def choose(flag, function, here, there):
    pl.when(flag == 1)(lambda: function(here, there))
    pl.when(flag == 0)(lambda: function(there, here))


class Stream:
    def __init__(self, pairs, sems, ahead):
        self.copies = [pltpu.make_async_copy(source, target, sems.at[i]) for i, (source, target) in enumerate(pairs)]
        self.started = self.waited = 0
        self.ahead = ahead
        self.fill()

    def fill(self):
        while self.started < min(len(self.copies), self.waited + self.ahead):
            self.copies[self.started].start()
            self.started += 1

    def wait(self, count):
        for _ in range(count):
            self.copies[self.waited].wait()
            self.waited += 1
        self.fill()


def piece_kernel(n_expert, n_edata, count, first_ref, expert_ref, place_ref, *refs):
    mine, theirs, (gate_hbm, up_hbm, down_hbm) = refs[:count], refs[count : 2 * count], refs[2 * count : 2 * count + 3]
    kept_ref, sent_ref, scaled_ref, share_ref = refs[2 * count + 3 : -12]
    rows_ref, grads_ref, lanes_ref, hidden_ref, act_ref, slope_ref, grad_gate_ref, grad_up_ref, gate_ref, up_ref, down_ref, sems = refs[-12:]
    width, units = gate_ref.shape
    pairs = []
    for at in range(0, units, TILE):
        columns = pl.ds(at, TILE)
        pairs.append((gate_hbm.at[0, :, columns], gate_ref.at[:, columns]))
        pairs.append((up_hbm.at[0, :, columns], up_ref.at[:, columns]))
    pairs += [(down_hbm.at[0, :, pl.ds(at, OUT_TILE)], down_ref.at[:, pl.ds(at, OUT_TILE)]) for at in range(0, width, OUT_TILE)]
    stream = Stream(pairs, sems, 4)

    def unpack(tokens, grads):
        at = 0
        for token, grad in zip(tokens, grads):
            block = slice(at, at + token.shape[0])
            rows_ref[block, :] = token[:, :width]
            grads_ref[block, :] = grad[:, :width]
            lanes_ref[block, :] = token[:, width:].astype(F32) + grad[:, width:].astype(F32)
            at += token.shape[0]

    choose(first_ref[0], unpack, mine, theirs)
    values = lanes_ref[...]
    lane = lax.broadcasted_iota(jnp.int32, values.shape, 1)
    expert = expert_ref[0]
    weight = jnp.where(lane == expert, 64.0, 0.0) + jnp.where(lane == expert + n_expert, 1.0, 0.0)
    whole = jnp.where(lane == 2 * n_expert, 256.0, 0.0) + jnp.where(lane == 2 * n_expert + 1, 1.0, 0.0)
    gate = jnp.sum(values * weight, axis=1, keepdims=True) / jnp.sum(values * whole, axis=1, keepdims=True)
    share = width // n_edata
    share_ref[...] = grads_ref[:, pl.ds(pl.multiple_of(place_ref[0] * share, LANES), share)]

    for at in range(0, units, TILE):
        columns = slice(at, at + TILE)
        stream.wait(2)
        gate_pre = dot(rows_ref[...], gate_ref[:, columns], ((1,), (0,)))
        up_pre = dot(rows_ref[...], up_ref[:, columns], ((1,), (0,)))
        sig_gate = jax.nn.sigmoid(gate_pre)
        act_gate = gate_pre * sig_gate
        hidden = (act_gate * up_pre).astype(BF16)
        hidden_ref[:, columns] = hidden
        scaled_ref[:, columns] = (hidden.astype(F32) * gate).astype(BF16)
        act_ref[:, columns] = act_gate * gate
        slope_ref[:, columns] = up_pre * sig_gate * (1.0 + gate_pre * (1.0 - sig_gate)) * gate
    for at in range(0, width, OUT_TILE):
        columns = slice(at, at + OUT_TILE)
        stream.wait(1)
        rows_ref[:, columns] = (dot(hidden_ref[...], down_ref[:, columns], ((1,), (0,))) * gate).astype(BF16)
    for at in range(0, units, TILE):
        columns = slice(at, at + TILE)
        grad_hidden = dot(grads_ref[...], down_ref[columns, :], ((1,), (1,)))
        grad_gate_ref[:, columns] = (grad_hidden * slope_ref[:, columns]).astype(BF16)
        grad_up_ref[:, columns] = (grad_hidden * act_ref[:, columns]).astype(BF16)
    for at in range(0, width, OUT_TILE):
        columns = slice(at, at + OUT_TILE)
        grad = dot(grad_gate_ref[...], gate_ref[columns, :], ((1,), (1,)))
        grad = grad + dot(grad_up_ref[...], up_ref[columns, :], ((1,), (1,)))
        grads_ref[:, columns] = grad.astype(BF16)

    def give(own, other):
        own[...] = rows_ref[...]
        other[...] = grads_ref[...]

    choose(first_ref[0], give, kept_ref, sent_ref)


def piece(n_expert, n_edata, first, expert, place, mats, mine, theirs):
    width, units = mats[0].shape[1:]
    rows = sum(part.shape[0] for part in mine)
    vmem, smem, hbm = (pl.BlockSpec(memory_space=space) for space in (pltpu.VMEM, pltpu.SMEM, pltpu.HBM))
    outs = [(rows, width)] * 2 + [(rows, units), (rows, width // n_edata)]
    scratch = [((rows, width), BF16)] * 2 + [((rows, LANES), F32), ((rows, units), BF16)] + [((rows, units), F32)] * 2
    scratch += [((rows, units), BF16)] * 2 + [((width, units), BF16)] * 2 + [((units, width), BF16)]
    return pl.pallas_call(
        functools.partial(piece_kernel, n_expert, n_edata, len(mine)),
        out_shape=[jax.ShapeDtypeStruct(shape, BF16) for shape in outs],
        in_specs=[smem] * 3 + [vmem] * (2 * len(mine)) + [hbm] * 3,
        out_specs=[vmem] * len(outs),
        scratch_shapes=[pltpu.VMEM(*shape) for shape in scratch] + [pltpu.SemaphoreType.DMA((2 * units // TILE + width // OUT_TILE,))],
        compiler_params=pltpu.CompilerParams(vmem_limit_bytes=rows * 88 * 1024),
        cost_estimate=pl.CostEstimate(flops=10**6, bytes_accessed=10**5, transcendentals=0),
    )(first, expert, place, *mine, *theirs, *[pltpu.with_memory_space_constraint(mat, pltpu.HBM) for mat in mats])


def cut_kernel(n_edata, first_ref, place_ref, *refs):
    out_refs = refs[-(n_edata - 1) :]
    blocks = refs[: -(n_edata - 1)]
    share = out_refs[0].shape[1]

    def cut(blocks, _):
        for step, out_ref in enumerate(out_refs, 1):
            columns, at = pl.ds(pl.multiple_of((place_ref[0] ^ step) * share, LANES), share), 0
            for block in blocks:
                out_ref[at : at + block.shape[0], :] = block[:, columns]
                at += block.shape[0]

    choose(first_ref[0], cut, blocks[: len(blocks) // 2], blocks[len(blocks) // 2 :])


def cut_shares(n_edata, first, place, here, there):
    rows, width = sum(part.shape[0] for part in here), here[0].shape[1] - LANES
    vmem, smem = (pl.BlockSpec(memory_space=space) for space in (pltpu.VMEM, pltpu.SMEM))
    return pl.pallas_call(
        functools.partial(cut_kernel, n_edata),
        out_shape=[jax.ShapeDtypeStruct((rows, width // n_edata), BF16)] * (n_edata - 1),
        in_specs=[smem] * 2 + [vmem] * (len(here) + len(there)),
        out_specs=[vmem] * (n_edata - 1),
        compiler_params=pltpu.CompilerParams(vmem_limit_bytes=LIMIT),
        cost_estimate=pl.CostEstimate(flops=10**6, bytes_accessed=10**5, transcendentals=0),
    )(first, place, *here, *there)


def total_of(*parts):
    return sum(part.astype(F32) for part in parts)


def share_kernel(counts, continued, *refs):
    out_ref, at, total = refs[-1], 0, None
    columns = pl.ds(pl.multiple_of(pl.program_id(0) * SHARE_TILE, SHARE_TILE), SHARE_TILE)
    for count in counts:
        grads = jnp.concatenate([ref[:, columns] for ref in refs[at : at + count]], axis=0)
        term = dot(grads, refs[at + count][...], ((0,), (0,)))
        total = term if total is None else total + term
        at += count + 1
    if continued:
        out_ref[...] = (total + refs[at][...])[:, None, :]
    else:
        out_ref[...] = total


def weight_share(groups, begun):
    operands = [array for grads, hidden in groups for array in (*grads, hidden)]
    share, units = groups[0][0][0].shape[1], groups[0][1].shape[1]
    specs = [pl.BlockSpec(memory_space=pltpu.VMEM)] * len(operands)
    plain = pl.BlockSpec((SHARE_TILE, units), lambda i: (i, 0))
    continued = begun is not None
    return pl.pallas_call(
        functools.partial(share_kernel, [len(grads) for grads, _ in groups], continued),
        out_shape=jax.ShapeDtypeStruct((share, 1, units) if continued else (share, units), F32),
        grid=(share // SHARE_TILE,),
        in_specs=specs + [plain] * continued,
        out_specs=pl.BlockSpec((SHARE_TILE, 1, units), lambda i: (i, 0, 0)) if continued else plain,
        compiler_params=pltpu.CompilerParams(vmem_limit_bytes=LIMIT),
        cost_estimate=pl.CostEstimate(flops=10**6, bytes_accessed=10**5, transcendentals=0),
    )(*operands, *([begun] if continued else []))


def shards(tokens, out_grad, routes, gate_codes, w_gate, w_up, w_down):
    rows, width = tokens.shape
    n_expert = lax.axis_size("expert")
    n_edata = lax.axis_size("edata")
    expert = lax.axis_index("expert").astype(jnp.int32)
    place = lax.axis_index("edata").astype(jnp.int32)
    first = expert % 2 == 0
    pick = lambda here, there: jnp.where(first, here, there)
    flags = [value.astype(jnp.int32).reshape(1) for value in (first, expert, place)]
    firsts = list(range(8, n_expert, 8))
    n_first = len(firsts)
    core = lambda part: swap(part, "expert", 1)
    across = lambda part: swap(part, "expert", 2)

    own, sent = pick(tokens, out_grad), pick(out_grad, tokens)
    got = core(sent)
    order = Order(got)
    lanes = gate_lanes(routes, gate_codes, n_expert)
    block = order(make_block, flags[0], own, got, lanes)
    beside = across(block)
    straight_1 = [swap(block, "expert", step) for step in firsts]
    near_own = swap(block, "expert", 4)
    near_beside = swap(after(beside, *straight_1), "expert", 4)
    across_1 = [across(part) for part in straight_1]
    straight_2 = [swap(part, "expert", 4) for part in straight_1]
    near_own = after(near_own, *straight_1)
    straight_2 = after_all(straight_2, near_own)
    near_beside = after(near_beside, *straight_2)
    across_2 = [across(part) for part in straight_2]
    across_1 = after_all(across_1, *straight_2)
    across_2 = after_all(across_2, near_beside)
    pieces_1 = [block, beside, *straight_1, *across_1]
    pieces_2 = [near_own, near_beside, *straight_2, *across_2]
    got_2 = [core(part) for part in pieces_2]
    got_1 = list(after_all([core(part) for part in pieces_1], *got_2))
    run = lambda *parts: piece(n_expert, n_edata, *flags, (w_gate, w_up, w_down), parts[: len(parts) // 2], parts[len(parts) // 2 :])
    size = 2 * rows
    cuts = lambda total, count: [total[i * size : (i + 1) * size] for i in range(count)]
    add = lambda *a: tuple(a[i] + a[len(a) // 2 + i] for i in range(len(a) // 2))

    cuts_out = order(lambda *a: cut_shares(n_edata, flags[0], flags[2], a[: len(pieces_1)], a[len(pieces_1) :]), *got_1, *pieces_2)
    mine = [swap(part, "edata", step) for step, part in enumerate(cuts_out, 1)]
    kept_1, sent_1, scaled_1, share_1 = order(run, *pieces_1, *got_1)
    scaled_other_1 = [swap(scaled_1, "edata", step) for step in range(1, n_edata)]
    parts_1 = order(lambda kept, got: cuts(kept + got, 2 + 2 * n_first), kept_1, core(sent_1))
    crossed_1 = [across(part) for part in parts_1[2 + n_first :]]
    kept_2, sent_2, scaled_2, share_2 = order(run, *pieces_2, *got_2)
    scaled_other_2 = [swap(scaled_2, "edata", step) for step in range(1, n_edata)]
    mine = after_all(mine, kept_2)
    ready_1 = order(add, *after_all(parts_1[2 : 2 + n_first], *mine), *crossed_1)
    back_1 = [swap(part, "expert", step) for part, step in zip(ready_1, firsts)]
    sent_2 = core(after(sent_2, *ready_1))
    near_2, *parts_2 = order(lambda kept, got: ((kept + got)[: 2 * size], *cuts((kept + got)[2 * size :], 2 * n_first)), kept_2, sent_2)
    crossed_2 = [across(part) for part in parts_2[n_first:]]
    back_near = swap(near_2, "expert", 4)
    theirs = [core(after(part, near_2)) for part in mine]
    own_share = order(lambda *a: weight_share([([a[0]], a[1]), ([a[2]], a[3])], None), share_1, scaled_1, share_2, scaled_2)
    ready_2 = order(add, *after_all(parts_2[:n_first], *after_all(scaled_other_1, own_share), *theirs), *crossed_2)
    back_2 = [swap(part, "expert", step + 4) for part, step in zip(ready_2, firsts)]
    ready = order(lambda part, got: part + got[size:], parts_1[1], after(back_near, *back_1))
    back_pair = across(ready)
    others = []
    for step in range(1, n_edata):
        here, there = mine[step - 1], theirs[step - 1]
        others += [([pick(here, there)], scaled_other_1[step - 1]), ([pick(there, here)], after(scaled_other_2[step - 1], ready))]
    grad_down = weight_share(others, own_share)
    order.last = grad_down
    total = order(lambda own, near, *parts: total_of(own, near[:size], *parts), parts_1[0], back_near, *back_1, *back_2)
    total = order(lambda total, pair: (total + pair.astype(F32)).astype(BF16), total, back_pair)
    kept, sent = pick(total[:rows], total[rows:]), pick(total[rows:], total[:rows])
    got = core(sent)
    return pick(kept, got), pick(got, kept), grad_down


def solution(mesh):
    by_token = P(("expert", "edata"), None)
    by_expert = P("expert", None, None)
    return jax.shard_map(
        shards,
        mesh=mesh,
        in_specs=(by_token,) * 4 + (by_expert,) * 3,
        out_specs=(by_token, by_token, P("edata", "expert", None)),
        check_vma=False,
    )
```

```python
import functools

import jax
import jax.numpy as jnp
from jax import lax
from jax.experimental import pallas as pl
from jax.experimental.pallas import tpu as pltpu
from jax.sharding import PartitionSpec as P

TILE = 256
OUT_TILE = 1024
SHARE_TILE = 256
LANES = 128
LIMIT = 12 * 1024 * 1024
BF16 = jnp.bfloat16
F32 = jnp.float32


def swap(value, axis, distance):
    size = lax.axis_size(axis)
    return lax.ppermute(value, axis, [(i, i ^ distance) for i in range(size)])


def after(value, *earlier):
    return lax.optimization_barrier((value,) + earlier)[0]


def after_all(values, *earlier):
    return lax.optimization_barrier(tuple(values) + earlier)[: len(values)]


def dot(left, right, contract):
    return lax.dot_general(left, right, (contract, ((), ())), preferred_element_type=F32)


class Order:
    def __init__(self, first):
        self.last = first

    def __call__(self, function, *operands):
        operands = lax.optimization_barrier((*operands, self.last))[:-1]
        result = function(*operands)
        self.last = result[0] if isinstance(result, (tuple, list)) else result
        return result


def gate_lanes(routes, gate_codes, n_expert):
    experts = jnp.arange(n_expert, dtype=jnp.int32)
    chosen = routes[:, :, None] == experts[None, None, :]
    codes = jnp.sum(jnp.where(chosen, gate_codes[:, :, None], 0), axis=1)
    total = jnp.sum(gate_codes, axis=1, keepdims=True)
    digits = jnp.concatenate([codes >> 6, codes & 63, total >> 8, total & 255], axis=1)
    return jnp.pad(digits, ((0, 0), (0, LANES - digits.shape[1]))).astype(BF16)


def block_kernel(first_ref, own_ref, got_ref, lanes_ref, out_ref):
    rows, width = own_ref.shape

    def fill(own, got):
        out_ref[own, :width] = own_ref[...]
        out_ref[got, :width] = got_ref[...]
        out_ref[own, width:] = lanes_ref[...]
        out_ref[got, width:] = jnp.zeros(lanes_ref.shape, BF16)

    choose(first_ref[0], fill, slice(0, rows), slice(rows, 2 * rows))


def make_block(first, own, got, lanes):
    rows, width = own.shape
    vmem = pl.BlockSpec(memory_space=pltpu.VMEM)
    return pl.pallas_call(
        block_kernel,
        out_shape=jax.ShapeDtypeStruct((2 * rows, width + LANES), BF16),
        in_specs=[pl.BlockSpec(memory_space=pltpu.SMEM)] + [vmem] * 3,
        out_specs=vmem,
        compiler_params=pltpu.CompilerParams(vmem_limit_bytes=4 * 1024 * 1024),
        cost_estimate=pl.CostEstimate(flops=10**6, bytes_accessed=10**6, transcendentals=0),
    )(first, own, got, lanes)


def choose(flag, function, here, there):
    pl.when(flag == 1)(lambda: function(here, there))
    pl.when(flag == 0)(lambda: function(there, here))


class Stream:
    def __init__(self, pairs, sems, ahead):
        self.copies = [pltpu.make_async_copy(source, target, sems.at[i]) for i, (source, target) in enumerate(pairs)]
        self.started = self.waited = 0
        self.ahead = ahead
        self.fill()

    def fill(self):
        while self.started < min(len(self.copies), self.waited + self.ahead):
            self.copies[self.started].start()
            self.started += 1

    def wait(self, count):
        for _ in range(count):
            self.copies[self.waited].wait()
            self.waited += 1
        self.fill()


def piece_kernel(n_expert, n_edata, count, first_ref, expert_ref, place_ref, *refs):
    mine, theirs, (gate_hbm, up_hbm, down_hbm) = refs[:count], refs[count : 2 * count], refs[2 * count : 2 * count + 3]
    kept_refs, sent_refs, scaled_refs, share_refs = (refs[2 * count + 3 + 2 * i : 2 * count + 5 + 2 * i] for i in range(4))
    rows_ref, grads_ref, lanes_ref, hidden_ref, act_ref, slope_ref, grad_gate_ref, grad_up_ref, gate_ref, up_ref, down_ref, sems = refs[-12:]
    width, units = gate_ref.shape
    half = rows_ref.shape[0] // 2
    pairs = []
    for at in range(0, units, TILE):
        columns = pl.ds(at, TILE)
        pairs.append((gate_hbm.at[0, :, columns], gate_ref.at[:, columns]))
        pairs.append((up_hbm.at[0, :, columns], up_ref.at[:, columns]))
    pairs += [(down_hbm.at[0, :, pl.ds(at, OUT_TILE)], down_ref.at[:, pl.ds(at, OUT_TILE)]) for at in range(0, width, OUT_TILE)]

    def body(sources, targets):
        out_refs, grad_refs = targets
        stream = Stream(pairs, sems, 6)
        at = 0
        for token, grad in zip(*sources):
            block = slice(at, at + token.shape[0])
            rows_ref[block, :] = token[:, :width]
            grads_ref[block, :] = grad[:, :width]
            lanes_ref[block, :] = token[:, width:].astype(F32) + grad[:, width:].astype(F32)
            at += token.shape[0]
        values = lanes_ref[...]
        lane = lax.broadcasted_iota(jnp.int32, values.shape, 1)
        expert = expert_ref[0]
        weight = jnp.where(lane == expert, 64.0, 0.0) + jnp.where(lane == expert + n_expert, 1.0, 0.0)
        whole = jnp.where(lane == 2 * n_expert, 256.0, 0.0) + jnp.where(lane == 2 * n_expert + 1, 1.0, 0.0)
        gate = jnp.sum(values * weight, axis=1, keepdims=True) / jnp.sum(values * whole, axis=1, keepdims=True)
        share = share_refs[0].shape[1]
        columns = pl.ds(pl.multiple_of(place_ref[0] * share, LANES), share)
        share_refs[0][...] = grads_ref[:half, columns]
        share_refs[1][...] = grads_ref[half:, columns]

        for at in range(0, units, TILE):
            columns = slice(at, at + TILE)
            stream.wait(2)
            gate_pre = dot(rows_ref[...], gate_ref[:, columns], ((1,), (0,)))
            up_pre = dot(rows_ref[...], up_ref[:, columns], ((1,), (0,)))
            sig_gate = jax.nn.sigmoid(gate_pre)
            act_gate = gate_pre * sig_gate
            hidden = (act_gate * up_pre).astype(BF16)
            hidden_ref[:, columns] = hidden
            scaled = (hidden.astype(F32) * gate).astype(BF16)
            scaled_refs[0][:, columns] = scaled[:half]
            scaled_refs[1][:, columns] = scaled[half:]
            act_ref[:, columns] = act_gate * gate
            slope_ref[:, columns] = up_pre * sig_gate * (1.0 + gate_pre * (1.0 - sig_gate)) * gate
        for at in range(0, width, OUT_TILE):
            columns = slice(at, at + OUT_TILE)
            stream.wait(1)
            out = (dot(hidden_ref[...], down_ref[:, columns], ((1,), (0,))) * gate).astype(BF16)
            out_refs[0][:, columns] = out[:half]
            out_refs[1][:, columns] = out[half:]
        for at in range(0, units, TILE):
            columns = slice(at, at + TILE)
            grad_hidden = dot(grads_ref[...], down_ref[columns, :], ((1,), (1,)))
            grad_gate_ref[:, columns] = (grad_hidden * slope_ref[:, columns]).astype(BF16)
            grad_up_ref[:, columns] = (grad_hidden * act_ref[:, columns]).astype(BF16)
        for at in range(0, width, OUT_TILE):
            columns = slice(at, at + OUT_TILE)
            grad = dot(grad_gate_ref[...], gate_ref[columns, :], ((1,), (1,)))
            grad = (grad + dot(grad_up_ref[...], up_ref[columns, :], ((1,), (1,)))).astype(BF16)
            grad_refs[0][:, columns] = grad[:half]
            grad_refs[1][:, columns] = grad[half:]

    pl.when(first_ref[0] == 1)(lambda: body((mine, theirs), (kept_refs, sent_refs)))
    pl.when(first_ref[0] == 0)(lambda: body((theirs, mine), (sent_refs, kept_refs)))


def piece(n_expert, n_edata, first, expert, place, mats, mine, theirs):
    width, units = mats[0].shape[1:]
    rows = sum(part.shape[0] for part in mine)
    vmem, smem, hbm = (pl.BlockSpec(memory_space=space) for space in (pltpu.VMEM, pltpu.SMEM, pltpu.HBM))
    outs = [(rows // 2, size) for size in (width, width, units, width // n_edata) for _ in range(2)]
    scratch = [((rows, width), BF16)] * 2 + [((rows, LANES), F32), ((rows, units), BF16)] + [((rows, units), F32)] * 2
    scratch += [((rows, units), BF16)] * 2 + [((width, units), BF16)] * 2 + [((units, width), BF16)]
    return pl.pallas_call(
        functools.partial(piece_kernel, n_expert, n_edata, len(mine)),
        out_shape=[jax.ShapeDtypeStruct(shape, BF16) for shape in outs],
        in_specs=[smem] * 3 + [vmem] * (2 * len(mine)) + [hbm] * 3,
        out_specs=[vmem] * len(outs),
        scratch_shapes=[pltpu.VMEM(*shape) for shape in scratch] + [pltpu.SemaphoreType.DMA((2 * units // TILE + width // OUT_TILE,))],
        compiler_params=pltpu.CompilerParams(vmem_limit_bytes=(16 + 42 * rows // 1024) * 1024 * 1024),
        cost_estimate=pl.CostEstimate(flops=10**6, bytes_accessed=10**5, transcendentals=0),
    )(first, expert, place, *mine, *theirs, *[pltpu.with_memory_space_constraint(mat, pltpu.HBM) for mat in mats])


def cut_kernel(n_edata, first_ref, place_ref, *refs):
    out_refs = refs[-(n_edata - 1) :]
    blocks = refs[: -(n_edata - 1)]
    share = out_refs[0].shape[1]

    def cut(blocks, _):
        for step, out_ref in enumerate(out_refs, 1):
            columns, at = pl.ds(pl.multiple_of((place_ref[0] ^ step) * share, LANES), share), 0
            for block in blocks:
                out_ref[at : at + block.shape[0], :] = block[:, columns]
                at += block.shape[0]

    choose(first_ref[0], cut, blocks[: len(blocks) // 2], blocks[len(blocks) // 2 :])


def cut_shares(n_edata, first, place, here, there):
    rows, width = sum(part.shape[0] for part in here), here[0].shape[1] - LANES
    vmem, smem = (pl.BlockSpec(memory_space=space) for space in (pltpu.VMEM, pltpu.SMEM))
    return pl.pallas_call(
        functools.partial(cut_kernel, n_edata),
        out_shape=[jax.ShapeDtypeStruct((rows, width // n_edata), BF16)] * (n_edata - 1),
        in_specs=[smem] * 2 + [vmem] * (len(here) + len(there)),
        out_specs=[vmem] * (n_edata - 1),
        compiler_params=pltpu.CompilerParams(vmem_limit_bytes=LIMIT),
        cost_estimate=pl.CostEstimate(flops=10**6, bytes_accessed=10**5, transcendentals=0),
    )(first, place, *here, *there)


def total_of(*parts):
    return sum(part.astype(F32) for part in parts)


def share_kernel(counts, *refs):
    out_ref, at, total = refs[-1], 0, None
    columns = pl.ds(pl.multiple_of(pl.program_id(0) * SHARE_TILE, SHARE_TILE), SHARE_TILE)
    for count in counts:
        grads = jnp.concatenate([ref[:, columns] for ref in refs[at : at + count]], axis=0)
        term = dot(grads, refs[at + count][...], ((0,), (0,)))
        total = term if total is None else total + term
        at += count + 1
    out_ref[...] = total[:, None, :]


def weight_share(groups):
    operands = [array for grads, hidden in groups for array in (*grads, hidden)]
    share, units = groups[0][0][0].shape[1], groups[0][1].shape[1]
    specs = [pl.BlockSpec(memory_space=pltpu.VMEM)] * len(operands)
    return pl.pallas_call(
        functools.partial(share_kernel, [len(grads) for grads, _ in groups]),
        out_shape=jax.ShapeDtypeStruct((share, 1, units), F32),
        grid=(share // SHARE_TILE,),
        in_specs=specs,
        out_specs=pl.BlockSpec((SHARE_TILE, 1, units), lambda i: (i, 0, 0)),
        compiler_params=pltpu.CompilerParams(vmem_limit_bytes=LIMIT),
        cost_estimate=pl.CostEstimate(flops=10**6, bytes_accessed=10**5, transcendentals=0),
    )(*operands)


def shards(tokens, out_grad, routes, gate_codes, w_gate, w_up, w_down):
    rows, width = tokens.shape
    n_expert = lax.axis_size("expert")
    n_edata = lax.axis_size("edata")
    expert = lax.axis_index("expert").astype(jnp.int32)
    place = lax.axis_index("edata").astype(jnp.int32)
    first = expert % 2 == 0
    pick = lambda here, there: jnp.where(first, here, there)
    flags = [value.astype(jnp.int32).reshape(1) for value in (first, expert, place)]
    firsts = list(range(8, n_expert, 8))
    n_first = len(firsts)
    core = lambda part: swap(part, "expert", 1)
    across = lambda part: swap(part, "expert", 2)

    own, sent = pick(tokens, out_grad), pick(out_grad, tokens)
    got = core(sent)
    order = Order(got)
    lanes = gate_lanes(routes, gate_codes, n_expert)
    block = order(make_block, flags[0], own, got, lanes)
    beside = across(block)
    straight_1 = [swap(block, "expert", step) for step in firsts]
    near_own = swap(block, "expert", 4)
    near_beside = swap(after(beside, *straight_1), "expert", 4)
    across_1 = [across(part) for part in straight_1]
    straight_2 = [swap(part, "expert", 4) for part in straight_1]
    near_own = after(near_own, *straight_1)
    straight_2 = after_all(straight_2, near_own)
    near_beside = after(near_beside, *straight_2)
    across_2 = [across(part) for part in straight_2]
    across_1 = after_all(across_1, *straight_2)
    across_2 = after_all(across_2, near_beside)
    pieces_1 = [block, beside, *straight_1, *across_1]
    pieces_2 = [near_own, near_beside, *straight_2, *across_2]
    got_2 = [core(part) for part in pieces_2]
    got_1 = [core(part) for part in pieces_1]
    run = lambda *parts: piece(n_expert, n_edata, *flags, (w_gate, w_up, w_down), parts[: len(parts) // 2], parts[len(parts) // 2 :])
    size = 2 * rows
    cuts = lambda total, count: [total[i * size : (i + 1) * size] for i in range(count)]
    add = lambda *a: tuple(a[i] + a[len(a) // 2 + i] for i in range(len(a) // 2))

    cuts_out = order(lambda *a: cut_shares(n_edata, flags[0], flags[2], a[: len(pieces_1)], a[len(pieces_1) :]), *got_1, *pieces_2)
    mine = [swap(part, "edata", step) for step, part in enumerate(cuts_out, 1)]
    kept_1, kept_2, sent_1, sent_2, scaled_1, scaled_2, share_1, share_2 = order(run, *pieces_1, *pieces_2, *got_1, *got_2)
    scaled_other_1, scaled_other_2 = ([swap(scaled, "edata", step) for step in range(1, n_edata)] for scaled in (scaled_1, scaled_2))
    sums = lambda kept, got: cuts(kept + got, 2 + 2 * n_first)
    sent_1, sent_2 = after_all([sent_1, sent_2], *mine)
    got_2, got_1 = core(sent_2), core(sent_1)
    near_own, near_beside, *parts_2 = order(sums, kept_2, got_2)
    crossed_2 = [across(part) for part in parts_2[n_first:]]
    back_beside = swap(near_beside, "expert", 4)
    own, beside, *parts_1 = order(sums, kept_1, got_1)
    crossed_1 = [across(part) for part in parts_1[n_first:]]
    theirs = [core(part) for part in mine]
    ready_2 = order(add, *after_all(parts_2[:n_first], *theirs), *crossed_2)
    back_2 = [swap(part, "expert", 4) for part in ready_2]
    ready = order(lambda part, got: part + got, beside, back_beside)
    back_pair = across(ready)
    add_three = lambda *a: tuple(a[i] + a[n_first + i] + a[2 * n_first + i] for i in range(n_first))
    ready_1 = order(add_three, *after_all(parts_1[:n_first], *scaled_other_1), *crossed_1, *back_2)
    back_1 = [swap(part, "expert", step) for part, step in zip(ready_1, firsts)]
    back_own = swap(after(near_own, *ready_1), "expert", 4)
    groups = [([share_1], scaled_1), ([share_2], scaled_2)]
    for here, there, hidden_1, hidden_2 in zip(mine, theirs, scaled_other_1, scaled_other_2):
        groups += [([pick(here, there)], hidden_1), ([pick(there, here)], hidden_2)]
    grad_down = weight_share([(after_all(grads, *ready_1), hidden) for grads, hidden in groups])
    order.last = grad_down
    total = order(total_of, own, back_pair, *back_1)
    total = order(lambda *parts: total_of(*parts).astype(BF16), total, back_own)
    kept, sent = pick(total[:rows], total[rows:]), pick(total[rows:], total[:rows])
    got = core(sent)
    return pick(kept, got), pick(got, kept), grad_down


def solution(mesh):
    by_token = P(("expert", "edata"), None)
    by_expert = P("expert", None, None)
    return jax.shard_map(
        shards,
        mesh=mesh,
        in_specs=(by_token,) * 4 + (by_expert,) * 3,
        out_specs=(by_token, by_token, P("edata", "expert", None)),
        check_vma=False,
    )
```

```python
import functools

import jax
import jax.numpy as jnp
from jax import lax
from jax.experimental import pallas as pl
from jax.experimental.pallas import tpu as pltpu
from jax.sharding import PartitionSpec as P

TILE = 256
OUT_TILE = 1024
SHARE_TILE = 256
LANES = 128
LIMIT = 12 * 1024 * 1024
BF16 = jnp.bfloat16
F32 = jnp.float32


def swap(value, axis, distance):
    size = lax.axis_size(axis)
    return lax.ppermute(value, axis, [(i, i ^ distance) for i in range(size)])


def after(value, *earlier):
    return lax.optimization_barrier((value,) + earlier)[0]


def after_all(values, *earlier):
    return lax.optimization_barrier(tuple(values) + earlier)[: len(values)]


def dot(left, right, contract):
    return lax.dot_general(left, right, (contract, ((), ())), preferred_element_type=F32)


class Order:
    def __init__(self, first):
        self.last = first

    def __call__(self, function, *operands):
        operands = lax.optimization_barrier((*operands, self.last))[:-1]
        result = function(*operands)
        self.last = result[0] if isinstance(result, (tuple, list)) else result
        return result


def gate_lanes(routes, gate_codes, n_expert):
    experts = jnp.arange(n_expert, dtype=jnp.int32)
    chosen = routes[:, :, None] == experts[None, None, :]
    codes = jnp.sum(jnp.where(chosen, gate_codes[:, :, None], 0), axis=1)
    total = jnp.sum(gate_codes, axis=1, keepdims=True)
    digits = jnp.concatenate([codes >> 6, codes & 63, total >> 8, total & 255], axis=1)
    return jnp.pad(digits, ((0, 0), (0, LANES - digits.shape[1]))).astype(BF16)


def block_kernel(first_ref, own_ref, got_ref, lanes_ref, out_ref):
    rows, width = own_ref.shape

    def fill(own, got):
        out_ref[own, :width] = own_ref[...]
        out_ref[got, :width] = got_ref[...]
        out_ref[own, width:] = lanes_ref[...]
        out_ref[got, width:] = jnp.zeros(lanes_ref.shape, BF16)

    choose(first_ref[0], fill, slice(0, rows), slice(rows, 2 * rows))


def make_block(first, own, got, lanes):
    rows, width = own.shape
    vmem = pl.BlockSpec(memory_space=pltpu.VMEM)
    return pl.pallas_call(
        block_kernel,
        out_shape=jax.ShapeDtypeStruct((2 * rows, width + LANES), BF16),
        in_specs=[pl.BlockSpec(memory_space=pltpu.SMEM)] + [vmem] * 3,
        out_specs=vmem,
        compiler_params=pltpu.CompilerParams(vmem_limit_bytes=4 * 1024 * 1024),
        cost_estimate=pl.CostEstimate(flops=10**6, bytes_accessed=10**6, transcendentals=0),
    )(first, own, got, lanes)


def choose(flag, function, here, there):
    pl.when(flag == 1)(lambda: function(here, there))
    pl.when(flag == 0)(lambda: function(there, here))


class Stream:
    def __init__(self, pairs, sems, ahead):
        self.copies = [pltpu.make_async_copy(source, target, sems.at[i]) for i, (source, target) in enumerate(pairs)]
        self.started = self.waited = 0
        self.ahead = ahead
        self.fill()

    def fill(self):
        while self.started < min(len(self.copies), self.waited + self.ahead):
            self.copies[self.started].start()
            self.started += 1

    def wait(self, count):
        for _ in range(count):
            self.copies[self.waited].wait()
            self.waited += 1
        self.fill()


def piece_kernel(n_expert, n_edata, count, first_ref, expert_ref, place_ref, *refs):
    mine, theirs, (gate_hbm, up_hbm, down_hbm) = refs[:count], refs[count : 2 * count], refs[2 * count : 2 * count + 3]
    outs = refs[2 * count + 3 : -12]
    kept_refs, sent_refs, scaled_refs, share_refs = outs[:4], outs[4:8], outs[8:10], outs[10:]
    rows_ref, grads_ref, lanes_ref, hidden_ref, act_ref, slope_ref, grad_gate_ref, grad_up_ref, gate_ref, up_ref, down_ref, sems = refs[-12:]
    width, units = gate_ref.shape
    half = rows_ref.shape[0] // 2
    ranges, at = [], 0
    for ref in kept_refs:
        ranges.append(slice(at, at + ref.shape[0]))
        at += ref.shape[0]
    pairs = []
    for at in range(0, units, TILE):
        columns = pl.ds(at, TILE)
        pairs.append((gate_hbm.at[0, :, columns], gate_ref.at[:, columns]))
        pairs.append((up_hbm.at[0, :, columns], up_ref.at[:, columns]))
    pairs += [(down_hbm.at[0, :, pl.ds(at, OUT_TILE)], down_ref.at[:, pl.ds(at, OUT_TILE)]) for at in range(0, width, OUT_TILE)]

    def body(sources, targets):
        out_refs, grad_refs = targets
        stream = Stream(pairs, sems, 10)
        at = 0
        for token, grad in zip(*sources):
            block = slice(at, at + token.shape[0])
            rows_ref[block, :] = token[:, :width]
            grads_ref[block, :] = grad[:, :width]
            lanes_ref[block, :] = token[:, width:].astype(F32) + grad[:, width:].astype(F32)
            at += token.shape[0]
        values = lanes_ref[...]
        lane = lax.broadcasted_iota(jnp.int32, values.shape, 1)
        expert = expert_ref[0]
        weight = jnp.where(lane == expert, 64.0, 0.0) + jnp.where(lane == expert + n_expert, 1.0, 0.0)
        whole = jnp.where(lane == 2 * n_expert, 256.0, 0.0) + jnp.where(lane == 2 * n_expert + 1, 1.0, 0.0)
        gate = jnp.sum(values * weight, axis=1, keepdims=True) / jnp.sum(values * whole, axis=1, keepdims=True)
        share = share_refs[0].shape[1]
        columns = pl.ds(pl.multiple_of(place_ref[0] * share, LANES), share)
        share_refs[0][...] = grads_ref[:half, columns]
        share_refs[1][...] = grads_ref[half:, columns]

        for at in range(0, units, TILE):
            columns = slice(at, at + TILE)
            stream.wait(2)
            gate_pre = dot(rows_ref[...], gate_ref[:, columns], ((1,), (0,)))
            up_pre = dot(rows_ref[...], up_ref[:, columns], ((1,), (0,)))
            sig_gate = jax.nn.sigmoid(gate_pre)
            act_gate = gate_pre * sig_gate
            hidden = (act_gate * up_pre).astype(BF16)
            hidden_ref[:, columns] = hidden
            scaled = (hidden.astype(F32) * gate).astype(BF16)
            scaled_refs[0][:, columns] = scaled[:half]
            scaled_refs[1][:, columns] = scaled[half:]
            act_ref[:, columns] = act_gate * gate
            slope_ref[:, columns] = up_pre * sig_gate * (1.0 + gate_pre * (1.0 - sig_gate)) * gate
        for at in range(0, width, OUT_TILE):
            columns = slice(at, at + OUT_TILE)
            stream.wait(1)
            out = (dot(hidden_ref[...], down_ref[:, columns], ((1,), (0,))) * gate).astype(BF16)
            for ref, block in zip(out_refs, ranges):
                ref[:, columns] = out[block]
        for at in range(0, units, TILE):
            columns = slice(at, at + TILE)
            grad_hidden = dot(grads_ref[...], down_ref[columns, :], ((1,), (1,)))
            grad_gate_ref[:, columns] = (grad_hidden * slope_ref[:, columns]).astype(BF16)
            grad_up_ref[:, columns] = (grad_hidden * act_ref[:, columns]).astype(BF16)
        for at in range(0, width, OUT_TILE):
            columns = slice(at, at + OUT_TILE)
            grad = dot(grad_gate_ref[...], gate_ref[columns, :], ((1,), (1,)))
            grad = (grad + dot(grad_up_ref[...], up_ref[columns, :], ((1,), (1,)))).astype(BF16)
            for ref, block in zip(grad_refs, ranges):
                ref[:, columns] = grad[block]

    pl.when(first_ref[0] == 1)(lambda: body((mine, theirs), (kept_refs, sent_refs)))
    pl.when(first_ref[0] == 0)(lambda: body((theirs, mine), (sent_refs, kept_refs)))


def piece(n_expert, n_edata, first, expert, place, mats, mine, theirs):
    width, units = mats[0].shape[1:]
    rows = sum(part.shape[0] for part in mine)
    vmem, smem, hbm = (pl.BlockSpec(memory_space=space) for space in (pltpu.VMEM, pltpu.SMEM, pltpu.HBM))
    first_two = 2 * mine[0].shape[0]
    parts = [(first_two, width), (rows // 2 - first_two, width)] * 2
    outs = parts * 2 + [(rows // 2, size) for size in (units, width // n_edata) for _ in range(2)]
    scratch = [((rows, width), BF16)] * 2 + [((rows, LANES), F32), ((rows, units), BF16)] + [((rows, units), F32)] * 2
    scratch += [((rows, units), BF16)] * 2 + [((width, units), BF16)] * 2 + [((units, width), BF16)]
    return pl.pallas_call(
        functools.partial(piece_kernel, n_expert, n_edata, len(mine)),
        out_shape=[jax.ShapeDtypeStruct(shape, BF16) for shape in outs],
        in_specs=[smem] * 3 + [vmem] * (2 * len(mine)) + [hbm] * 3,
        out_specs=[vmem] * len(outs),
        scratch_shapes=[pltpu.VMEM(*shape) for shape in scratch] + [pltpu.SemaphoreType.DMA((2 * units // TILE + width // OUT_TILE,))],
        compiler_params=pltpu.CompilerParams(vmem_limit_bytes=(16 + 42 * rows // 1024) * 1024 * 1024),
        cost_estimate=pl.CostEstimate(flops=10**6, bytes_accessed=10**5, transcendentals=0),
    )(first, expert, place, *mine, *theirs, *[pltpu.with_memory_space_constraint(mat, pltpu.HBM) for mat in mats])


def cut_kernel(n_edata, first_ref, place_ref, *refs):
    out_refs = refs[-(n_edata - 1) :]
    blocks = refs[: -(n_edata - 1)]
    share = out_refs[0].shape[1]

    def cut(blocks, _):
        for step, out_ref in enumerate(out_refs, 1):
            columns, at = pl.ds(pl.multiple_of((place_ref[0] ^ step) * share, LANES), share), 0
            for block in blocks:
                out_ref[at : at + block.shape[0], :] = block[:, columns]
                at += block.shape[0]

    choose(first_ref[0], cut, blocks[: len(blocks) // 2], blocks[len(blocks) // 2 :])


def cut_shares(n_edata, first, place, here, there):
    rows, width = sum(part.shape[0] for part in here), here[0].shape[1] - LANES
    vmem, smem = (pl.BlockSpec(memory_space=space) for space in (pltpu.VMEM, pltpu.SMEM))
    return pl.pallas_call(
        functools.partial(cut_kernel, n_edata),
        out_shape=[jax.ShapeDtypeStruct((rows, width // n_edata), BF16)] * (n_edata - 1),
        in_specs=[smem] * 2 + [vmem] * (len(here) + len(there)),
        out_specs=[vmem] * (n_edata - 1),
        compiler_params=pltpu.CompilerParams(vmem_limit_bytes=LIMIT),
        cost_estimate=pl.CostEstimate(flops=10**6, bytes_accessed=10**5, transcendentals=0),
    )(first, place, *here, *there)


def total_of(*parts):
    return sum(part.astype(F32) for part in parts)


def share_kernel(counts, *refs):
    out_ref, at, total = refs[-1], 0, None
    columns = pl.ds(pl.multiple_of(pl.program_id(0) * SHARE_TILE, SHARE_TILE), SHARE_TILE)
    for count in counts:
        grads = jnp.concatenate([ref[:, columns] for ref in refs[at : at + count]], axis=0)
        term = dot(grads, refs[at + count][...], ((0,), (0,)))
        total = term if total is None else total + term
        at += count + 1
    out_ref[...] = total[:, None, :]


def weight_share(groups):
    operands = [array for grads, hidden in groups for array in (*grads, hidden)]
    share, units = groups[0][0][0].shape[1], groups[0][1].shape[1]
    specs = [pl.BlockSpec(memory_space=pltpu.VMEM)] * len(operands)
    return pl.pallas_call(
        functools.partial(share_kernel, [len(grads) for grads, _ in groups]),
        out_shape=jax.ShapeDtypeStruct((share, 1, units), F32),
        grid=(share // SHARE_TILE,),
        in_specs=specs,
        out_specs=pl.BlockSpec((SHARE_TILE, 1, units), lambda i: (i, 0, 0)),
        compiler_params=pltpu.CompilerParams(vmem_limit_bytes=LIMIT),
        cost_estimate=pl.CostEstimate(flops=10**6, bytes_accessed=10**5, transcendentals=0),
    )(*operands)


def shards(tokens, out_grad, routes, gate_codes, w_gate, w_up, w_down):
    rows, width = tokens.shape
    n_expert = lax.axis_size("expert")
    n_edata = lax.axis_size("edata")
    expert = lax.axis_index("expert").astype(jnp.int32)
    place = lax.axis_index("edata").astype(jnp.int32)
    first = expert % 2 == 0
    pick = lambda here, there: jnp.where(first, here, there)
    flags = [value.astype(jnp.int32).reshape(1) for value in (first, expert, place)]
    firsts = list(range(8, n_expert, 8))
    n_first = len(firsts)
    core = lambda part: swap(part, "expert", 1)
    across = lambda part: swap(part, "expert", 2)

    own, sent = pick(tokens, out_grad), pick(out_grad, tokens)
    got = core(sent)
    order = Order(got)
    lanes = gate_lanes(routes, gate_codes, n_expert)
    block = order(make_block, flags[0], own, got, lanes)
    beside = across(block)
    straight_1 = [swap(block, "expert", step) for step in firsts]
    near_own = swap(block, "expert", 4)
    near_beside = swap(after(beside, *straight_1), "expert", 4)
    across_1 = [across(part) for part in straight_1]
    straight_2 = [swap(part, "expert", 4) for part in straight_1]
    near_own = after(near_own, *straight_1)
    straight_2 = after_all(straight_2, near_own)
    near_beside = after(near_beside, *straight_2)
    across_2 = [across(part) for part in straight_2]
    across_1 = after_all(across_1, *straight_2)
    across_2 = after_all(across_2, near_beside)
    pieces_1 = [block, beside, *straight_1, *across_1]
    pieces_2 = [near_own, near_beside, *straight_2, *across_2]
    got_2 = [core(part) for part in pieces_2]
    got_1 = [core(part) for part in pieces_1]
    run = lambda *parts: piece(n_expert, n_edata, *flags, (w_gate, w_up, w_down), parts[: len(parts) // 2], parts[len(parts) // 2 :])
    size = 2 * rows
    cuts = lambda total, count: [total[i * size : (i + 1) * size] for i in range(count)]
    add = lambda *a: tuple(a[i] + a[len(a) // 2 + i] for i in range(len(a) // 2))

    cuts_out = order(lambda *a: cut_shares(n_edata, flags[0], flags[2], a[: len(pieces_1)], a[len(pieces_1) :]), *got_1, *pieces_2)
    mine = [swap(part, "edata", step) for step, part in enumerate(cuts_out, 1)]
    *sums_of, scaled_1, scaled_2, share_1, share_2 = order(run, *pieces_1, *pieces_2, *got_1, *got_2)
    scaled_other_1, scaled_other_2 = ([swap(scaled, "edata", step) for step in range(1, n_edata)] for scaled in (scaled_1, scaled_2))
    kept, sent = sums_of[:4], after_all(sums_of[4:], *mine)
    got_last, got_near = core(sent[3]), core(sent[2])
    sums = lambda kept, got: cuts(kept + got, kept.shape[0] // size)
    parts_2 = order(sums, kept[3], got_last)
    got_first, got_own = (core(part) for part in after_all([sent[1], sent[0]], *parts_2))
    crossed_2 = [across(part) for part in parts_2[n_first:]]
    near_own, near_beside = order(sums, kept[2], got_near)
    back_beside = swap(near_beside, "expert", 4)
    parts_1 = order(sums, kept[1], got_first)
    crossed_1 = [across(part) for part in parts_1[n_first:]]
    own, beside = order(sums, kept[0], got_own)
    theirs = [core(part) for part in mine]
    ready_2 = order(add, *after_all(parts_2[:n_first], *theirs), *crossed_2)
    back_2 = [swap(part, "expert", 4) for part in ready_2]
    ready = order(lambda part, got: part + got, beside, back_beside)
    add_three = lambda *a: tuple(a[i] + a[n_first + i] + a[2 * n_first + i] for i in range(n_first))
    ready_1 = order(add_three, *after_all(parts_1[:n_first], *scaled_other_1), *crossed_1, *back_2)
    back_1 = [swap(part, "expert", step) for part, step in zip(ready_1, firsts)]
    back_pair = across(after(ready, *ready_1))
    back_own = swap(after(near_own, *ready_1), "expert", 4)
    groups = [([share_1], scaled_1), ([share_2], scaled_2)]
    for here, there, hidden_1, hidden_2 in zip(mine, theirs, scaled_other_1, scaled_other_2):
        groups += [([pick(here, there)], hidden_1), ([pick(there, here)], hidden_2)]
    grad_down = weight_share([(after_all(grads, *ready_1), hidden) for grads, hidden in groups])
    order.last = grad_down
    total = order(total_of, own, back_own)
    total = order(lambda *parts: total_of(*parts).astype(BF16), total, back_pair, *back_1)
    kept, sent = pick(total[:rows], total[rows:]), pick(total[rows:], total[:rows])
    got = core(sent)
    return pick(kept, got), pick(got, kept), grad_down


def solution(mesh):
    by_token = P(("expert", "edata"), None)
    by_expert = P("expert", None, None)
    return jax.shard_map(
        shards,
        mesh=mesh,
        in_specs=(by_token,) * 4 + (by_expert,) * 3,
        out_specs=(by_token, by_token, P("edata", "expert", None)),
        check_vma=False,
    )
```
